32 devices in a mesh: row: 4 (over y, x), col: 8 (over z, core).
Axes of the slice: x: 2, y: 2, z: 4, core: 2. Of those that a mesh axis runs over, the one named last changes fastest.
Arguments:
- amplitudes: float32 [64, 64, 3072], P('row', None, 'col'), may hold values from -6 to 6
- integrals: float32 [3072, 800], P('col'), may hold values from -0.21875 to 0.21875
- occ_irrep: int32 [64], replicated, may hold values from 0 to 7, as said below
- cd_irrep: int32 [3072], P('col'), may hold values from 0 to 7, as said below
Outputs:
- residual: float32 [4096, 800], P(('row', 'col'))
The draws below stay inside these ranges and needn't reach their ends.
Inputs may be any that keep to these rules, and one draw needn't show every extreme that they name: `occ_irrep`: D2h irrep labels; the orbitals are sorted by irrep: labels never fall along the orbitals, and every label occurs. `cd_irrep`: D2h irrep labels of the pairs; within each aligned block of 384 pairs the labels never fall and every label occurs.
All inputs are finite; a program needn't handle non-finite values.
Results may differ from the reference program's by a relative error of at most 0.0001.
Values sent between devices are 32-bit elements; how exact they have to be, the bound alone decides.
A program may use at most 64 MiB of HBM per device.

```python
import math
import jax
import jax.numpy as jnp
from jax import lax

OCC = 64
CDL = 384
AB = 800
CD = 3072


def sorted_runs(key, length):
    shuffled = jax.random.permutation(key, length - 1) + 1
    boundaries = jnp.sort(shuffled[:7])
    places = jnp.arange(length)
    return jnp.sum((places[:, None] >= boundaries[None, :]).astype(jnp.int32), axis=1).astype(jnp.int32)


def draw_occ_irrep(key, part):
    key = jax.random.fold_in(key, 11)
    return sorted_runs(key, OCC)


def draw_cd_irrep(key, part):
    key = jax.random.fold_in(key, 23)
    shard_keys = jax.random.split(key, CD // CDL)
    labels = jax.vmap(lambda single: sorted_runs(single, CDL))(shard_keys)
    return labels.reshape(CD).astype(jnp.int32)


def level_of(key, shape, pieces, smallest, high):
    def one(axis_at, parts):
        steps = jax.random.uniform(jax.random.fold_in(jax.random.fold_in(key, 6), axis_at), (parts,), jnp.float32, smallest / len(pieces), high / len(pieces))
        return jnp.repeat(jnp.exp(steps), shape[axis_at] // parts).reshape((-1,) + (1,) * (len(shape) - axis_at - 1))

    factor_of = one(*pieces[0])
    for cut in pieces[1:]:
        factor_of = factor_of * one(*cut)
    return factor_of


def gaussian(rng, extent, deviation, reach, cuts=(), kind=jnp.bfloat16):
    loudness = level_of(rng, extent, cuts, -0.22, 0.18) if cuts else 1.0
    array = jax.random.normal(rng, extent, jnp.float32) * deviation * loudness
    return jnp.minimum(jnp.maximum(array, -reach), reach).astype(kind)


def setup_inputs(seed: int = 0) -> dict:
    streams_of = jax.random.split(jax.random.key(seed), 5)
    return {
        "amplitudes": gaussian(streams_of[0], (OCC, OCC, CD), 1.0, 6.0, ((0, 4), (2, 8)), jnp.float32),
        "integrals": gaussian(streams_of[1], (CD, AB), (CD // 4) ** -0.5, 0.21875, ((0, 8),), jnp.float32),
        "occ_irrep": draw_occ_irrep(jax.random.fold_in(streams_of[4], 71), 0),
        "cd_irrep": draw_cd_irrep(jax.random.fold_in(streams_of[4], 71), 0),
    }


def reference(amplitudes, integrals, occ_irrep, cd_irrep):
    occupied = amplitudes.shape[0]
    pair_sym = jnp.bitwise_xor(occ_irrep[:, None], occ_irrep[None, :])
    width = math.gcd(CD, 4096)
    accum = jnp.zeros((occupied * occupied, integrals.shape[1]), jnp.float32)
    for offset in range(0, CD, width):
        piece = amplitudes[:, :, offset:offset + width]
        labels = cd_irrep[offset:offset + width]
        allowed = pair_sym[:, :, None] == labels[None, None, :]
        combined = jnp.where(allowed, piece + jnp.swapaxes(piece, 0, 1), jnp.float32(0.0))
        accum = accum + jnp.dot(combined.reshape(occupied * occupied, width), integrals[offset:offset + width], precision=lax.Precision.HIGHEST, preferred_element_type=jnp.float32)
    return accum
```

```python
import jax
import jax.numpy as jnp
from jax import lax
from jax.experimental import pallas as pl
from jax.experimental.pallas import tpu as pltpu
from jax.sharding import PartitionSpec as P

MESH = pl.DeviceIdType.MESH
BLOCKS = 9


def plain_body(amplitudes, integrals, occ_irrep, cd_irrep):
    own_count = amplitudes.shape[0]
    occupied = amplitudes.shape[1]
    received = lax.all_to_all(amplitudes, "row", split_axis=1, concat_axis=0, tiled=True)
    mirrored = jnp.swapaxes(received, 0, 1)
    first_i = lax.axis_index("row") * own_count
    own_irrep = lax.dynamic_slice_in_dim(occ_irrep, first_i, own_count, 0)
    pair_sym = jnp.bitwise_xor(own_irrep[:, None], occ_irrep[None, :])
    allowed = pair_sym[:, :, None] == cd_irrep[None, None, :]
    combined = jnp.where(allowed, amplitudes + mirrored, jnp.float32(0.0))
    combined = combined.reshape(own_count * occupied, amplitudes.shape[2])
    partial_value = jnp.dot(
        combined, integrals, precision=lax.Precision.HIGHEST, preferred_element_type=jnp.float32
    )
    return lax.psum_scatter(partial_value, "col", scatter_dimension=0, tiled=True)


def split(value):
    high = value.astype(jnp.bfloat16)
    low = (value - high.astype(jnp.float32)).astype(jnp.bfloat16)
    return high, low


def kernel(
    amp, vt, occ_s, occ_v, lab, out,
    land, lhs, rhs, part, core_in, own, from_left, from_right, to_right, to_left,
    final, sib, gsend, grecv, gsib,
    a2a_s, a2a_r, loc, core_s, core_r, right_s, right_r, left_s, left_r, sib_s, sib_r, g_s, g_r, gs_s, gs_r,
):
    a, c = lax.axis_index("row"), lax.axis_index("col")
    z, core = lax.div(c, 2), lax.rem(c, 2)
    other = 1 - core
    sibling = (a, 2 * z + other)
    a_hi, a_lo = lax.div(a, 2), lax.rem(a, 2)
    peers = [a, 2 * a_hi + 1 - a_lo, 2 * (1 - a_hi) + a_lo, 2 * (1 - a_hi) + 1 - a_lo]
    flips = [None, a_lo, a_hi, a_hi]

    def flip(h, s):
        return s if h == 0 else 1 - s

    def octet(index):
        return pl.ds(pl.multiple_of(8 * index, 8), 8)

    barrier = pltpu.get_barrier_semaphore()
    pl.semaphore_signal(barrier, 1, device_id=sibling, device_id_type=MESH)
    for t in (1, 2, 3):
        pl.semaphore_signal(barrier, 1, device_id=(peers[t], c), device_id_type=MESH)

    @pl.when(z > 0)
    def _():
        pl.semaphore_signal(barrier, 1, device_id=(a, c - 2), device_id_type=MESH)

    @pl.when(z < 3)
    def _():
        pl.semaphore_signal(barrier, 1, device_id=(a, c + 2), device_id_type=MESH)

    @pl.when((z == 0) | (z == 3))
    def _():
        pl.semaphore_wait(barrier, 5)

    @pl.when((z == 1) | (z == 2))
    def _():
        pl.semaphore_wait(barrier, 6)

    exchanged = {}
    for t in (3, 1, 2):
        for h in (0, 1):
            n = 2 * (t - 1) + h
            theirs = 1 - flips[t]
            copy = pltpu.make_async_remote_copy(
                src_ref=amp.at[octet(flip(h, theirs)), octet(2 * peers[t] + h), :],
                dst_ref=land.at[n], send_sem=a2a_s.at[n], recv_sem=a2a_r.at[n],
                device_id=(peers[t], c), device_id_type=MESH,
            )
            copy.start()
            exchanged[n] = copy
    local = {}
    for n, (first, second) in ((6, (0, 0)), (7, (1, 1)), (8, (1, 0))):
        copy = pltpu.make_async_copy(
            amp.at[8 * first:8 * first + 8, octet(2 * a + second), :], land.at[n], loc.at[n - 6]
        )
        copy.start()
        local[n] = copy

    depth = vt.shape[1]
    v_high, v_low = split(vt[...])
    rhs[:, 0:depth] = v_high
    rhs[:, depth:2 * depth] = v_low
    rhs[:, 2 * depth:3 * depth] = v_high
    labels = lab[...]

    def block(n):
        if n < 6:
            t, h = n // 2 + 1, n % 2
            exchanged[n].wait_recv()
            own_oct, col = h, 2 * peers[t] + flip(h, flips[t])
        else:
            local[n].wait()
            own_oct = 0 if n == 8 else n - 6
            col = 2 * a + (1 if n == 8 else n - 6)
        column_sym = occ_v[octet(col), :]
        for i in range(8):
            row = 8 * own_oct + i
            pair_sym = jnp.bitwise_xor(column_sym, occ_s[16 * a + row])
            total = amp[row, octet(col), :] + land[n, :, i, :]
            total = jnp.where(pair_sym == labels, total, jnp.float32(0.0))
            high, low = split(total)
            lhs[8 * i:8 * i + 8, 0:depth] = high.astype(jnp.float32)
            lhs[8 * i:8 * i + 8, depth:2 * depth] = low.astype(jnp.float32)
        high = lhs[:, 0:depth].astype(jnp.bfloat16)
        low = lhs[:, depth:2 * depth].astype(jnp.bfloat16)
        stacked = jnp.concatenate([high, high, low], axis=1)
        product = lax.dot_general(
            stacked, rhs[...], (((1,), (1,)), ((), ())), preferred_element_type=jnp.float32
        )
        part[n] = product.reshape(8, 8, product.shape[1])
        copy = pltpu.make_async_remote_copy(
            src_ref=part.at[n, pl.ds(4 * other, 4)], dst_ref=core_in.at[n],
            send_sem=core_s.at[n], recv_sem=core_r.at[n], device_id=sibling, device_id_type=MESH,
        )
        copy.start()
        return copy

    order = (6, 7, 8, 2, 3, 0, 1, 4, 5)

    def chain(n, source, sems, target):
        return pltpu.make_async_remote_copy(
            src_ref=source.at[n], dst_ref=(from_left if sems == "right" else from_right).at[n],
            send_sem=(right_s if sems == "right" else left_s).at[n],
            recv_sem=(right_r if sems == "right" else left_r).at[n],
            device_id=target, device_id_type=MESH,
        )

    def right(n, source):
        return chain(n, source, "right", (a, lax.rem(c + 2, 8)))

    def left(n, source):
        return chain(n, source, "left", (a, lax.rem(c + 6, 8)))

    core_copies = {}
    previous = None

    def gather(n):
        core_copies[n].wait_recv()
        own[n] = part[n, pl.ds(4 * core, 4)] + core_in[n]

        @pl.when(z == 0)
        def _():
            right(n, own).start()

        @pl.when(z == 3)
        def _():
            left(n, own).start()

    for n in order:
        core_copies[n] = block(n)
        if previous is not None:
            gather(previous)
        previous = n
    gather(previous)

    def pass_right(n):
        right(n, to_right).wait_recv()
        to_right[n] = own[n] + from_left[n]
        right(n, to_right).start()

    def pass_left(n):
        left(n, to_left).wait_recv()
        to_left[n] = own[n] + from_right[n]
        left(n, to_left).start()

    lag = 2

    @pl.when(z == 0)
    def _():
        for n in order:
            left(n, own).wait_recv()
            final[n] = own[n] + from_right[n]
        for n in order:
            right(n, own).wait_send()

    @pl.when(z == 3)
    def _():
        for n in order:
            right(n, own).wait_recv()
            final[n] = own[n] + from_left[n]
        for n in order:
            left(n, own).wait_send()

    @pl.when(z == 1)
    def _():
        for q in range(BLOCKS + lag):
            if q < BLOCKS:
                pass_right(order[q])
            if q >= lag:
                n = order[q - lag]
                pass_left(n)
                final[n] = to_right[n] + from_right[n]
        for n in order:
            right(n, to_right).wait_send()
            left(n, to_left).wait_send()

    @pl.when(z == 2)
    def _():
        for q in range(BLOCKS + lag):
            if q < BLOCKS:
                pass_left(order[q])
            if q >= lag:
                n = order[q - lag]
                pass_right(n)
                final[n] = to_left[n] + from_left[n]
        for n in order:
            right(n, to_right).wait_send()
            left(n, to_left).wait_send()

    half, odd = lax.div(z, 2), lax.rem(z, 2)
    ends = []
    g_copies = {}
    for t in (3, 1, 2):
        s = flips[t]
        h = half + s - 2 * half * s
        value = final[2 * (t - 1) + h]
        for q in range(2):
            rows = [
                jnp.where(odd == 1, value[2 * q + e, 4:8, :], value[2 * q + e, 0:4, :]) for e in (0, 1)
            ]
            gsend[t - 1, q] = jnp.concatenate(rows, axis=0)
        copy = pltpu.make_async_remote_copy(
            src_ref=gsend.at[t - 1], dst_ref=grecv.at[t - 1], send_sem=g_s.at[t - 1],
            recv_sem=g_r.at[t - 1], device_id=(peers[t], c), device_id_type=MESH,
        )
        copy.start()
        g_copies[t] = copy
    for slot in range(5):
        index = (2 * slot + half) if slot < 4 else 8
        copy = pltpu.make_async_remote_copy(
            src_ref=final.at[index], dst_ref=sib.at[slot], send_sem=sib_s.at[slot],
            recv_sem=sib_r.at[slot], device_id=sibling, device_id_type=MESH,
        )
        copy.start()
        ends.append(copy)
    for copy in ends:
        copy.wait_recv()

    def direct(slot, il):
        mine = final[(2 * slot + half) if slot < 4 else 8, 2 * core + il]
        theirs = sib[slot, 2 * core + il]
        return jnp.where(odd == core, mine, theirs)

    for il in range(2):
        for t in (1, 2, 3):
            s = flips[t]
            out[il, octet(2 * peers[t] + (half + s - 2 * half * s)), :] = direct(t - 1, il)
        out[il, octet(2 * a + half), :] = direct(3, il)
        straight = direct(4, il)
        rows = []
        for j in range(8):
            def pick(ref_row):
                options = [ref_row[4 * o + 2 * k + il:4 * o + 2 * k + il + 1, :] for o in (0, 1) for k in (0, 1)]
                even = jnp.where(core == 1, options[1], options[0])
                uneven = jnp.where(core == 1, options[3], options[2])
                return jnp.where(odd == 1, uneven, even)
            mine, theirs = pick(final[8, j % 4]), pick(sib[4, j % 4])
            rows.append(jnp.where(core == j // 4, mine, theirs))
        turned = jnp.concatenate(rows, axis=0)
        out[il, octet(2 * a + 1 - half), :] = jnp.where(half == 0, straight, turned)

    g_sib = {}
    for t in (3, 1, 2):
        g_copies[t].wait_recv()
        copy = pltpu.make_async_remote_copy(
            src_ref=grecv.at[t - 1], dst_ref=gsib.at[t - 1], send_sem=gs_s.at[t - 1],
            recv_sem=gs_r.at[t - 1], device_id=sibling, device_id_type=MESH,
        )
        copy.start()
        g_sib[t] = copy
    for t in (3, 1, 2):
        g_sib[t].wait_recv()
        s = flips[t]
        g = 1 - (half + s - 2 * half * s)
        for il in range(2):
            rows = []
            for j in range(8):
                q, e = (j % 4) // 2, j % 2

                def pick(tile):
                    low = tile[4 * e + il:4 * e + il + 1, :]
                    high = tile[4 * e + 2 + il:4 * e + 3 + il, :]
                    return jnp.where(core == 1, high, low)
                mine, theirs = pick(grecv[t - 1, q]), pick(gsib[t - 1, q])
                rows.append(jnp.where(core == j // 4, mine, theirs))
            out[il, octet(2 * peers[t] + g), :] = jnp.concatenate(rows, axis=0)

    for n in range(6):
        exchanged[n].wait_send()
    for n in range(BLOCKS):
        core_copies[n].wait_send()
    for copy in ends:
        copy.wait_send()
    for t in (1, 2, 3):
        g_copies[t].wait_send()
        g_sib[t].wait_send()


def paired_body(amplitudes, integrals, occ_irrep, cd_irrep):
    depth, width = integrals.shape
    vmem = pl.BlockSpec(memory_space=pltpu.VMEM)
    smem = pl.BlockSpec(memory_space=pltpu.SMEM)
    f32 = jnp.float32

    def sums(count):
        return pltpu.VMEM((count, 4, 8, width), f32)

    def sems(count):
        return [pltpu.SemaphoreType.DMA((count,))] * 2

    result = pl.pallas_call(
        kernel,
        out_shape=jax.ShapeDtypeStruct((2, 64, width), f32),
        in_specs=[vmem, vmem, smem, vmem, vmem],
        out_specs=vmem,
        scratch_shapes=[
            pltpu.VMEM((BLOCKS, 8, 8, depth), f32),
            pltpu.VMEM((64, 2 * depth), f32),
            pltpu.VMEM((width, 3 * depth), jnp.bfloat16),
            pltpu.VMEM((BLOCKS, 8, 8, width), f32),
            sums(BLOCKS), sums(BLOCKS), sums(BLOCKS), sums(BLOCKS), sums(BLOCKS), sums(BLOCKS),
            sums(BLOCKS), sums(5),
            pltpu.VMEM((3, 2, 8, width), f32),
            pltpu.VMEM((3, 2, 8, width), f32),
            pltpu.VMEM((3, 2, 8, width), f32),
            *sems(6), pltpu.SemaphoreType.DMA((3,)),
            *sems(BLOCKS), *sems(BLOCKS), *sems(BLOCKS), *sems(5), *sems(3), *sems(3),
        ],
        compiler_params=pltpu.CompilerParams(
            collective_id=0, has_side_effects=True, vmem_limit_bytes=50 << 20
        ),
    )(amplitudes, integrals.T, occ_irrep, occ_irrep.reshape(64, 1), cd_irrep.reshape(1, depth))
    return result.reshape(128, width)


def solution(mesh):
    in_specs = (P("row", None, "col"), P("col", None), P(), P("col"))
    out_specs = P(("row", "col"), None)
    fits = mesh.shape["row"] == 4 and mesh.shape["col"] == 8

    def body(amplitudes, integrals, occ_irrep, cd_irrep):
        paired = fits and amplitudes.shape[:2] == (16, 64)
        chosen = paired_body if paired else plain_body
        return chosen(amplitudes, integrals, occ_irrep, cd_irrep)

    return jax.shard_map(body, mesh=mesh, in_specs=in_specs, out_specs=out_specs, check_vma=False)
```

```python
import jax
import jax.numpy as jnp
from jax import lax
from jax.experimental import pallas as pl
from jax.experimental.pallas import tpu as pltpu
from jax.sharding import PartitionSpec as P

MESH = pl.DeviceIdType.MESH
BLOCKS = 9


def plain_body(amplitudes, integrals, occ_irrep, cd_irrep):
    own_count = amplitudes.shape[0]
    occupied = amplitudes.shape[1]
    received = lax.all_to_all(amplitudes, "row", split_axis=1, concat_axis=0, tiled=True)
    mirrored = jnp.swapaxes(received, 0, 1)
    first_i = lax.axis_index("row") * own_count
    own_irrep = lax.dynamic_slice_in_dim(occ_irrep, first_i, own_count, 0)
    pair_sym = jnp.bitwise_xor(own_irrep[:, None], occ_irrep[None, :])
    allowed = pair_sym[:, :, None] == cd_irrep[None, None, :]
    combined = jnp.where(allowed, amplitudes + mirrored, jnp.float32(0.0))
    combined = combined.reshape(own_count * occupied, amplitudes.shape[2])
    partial_value = jnp.dot(
        combined, integrals, precision=lax.Precision.HIGHEST, preferred_element_type=jnp.float32
    )
    return lax.psum_scatter(partial_value, "col", scatter_dimension=0, tiled=True)


def split(value):
    high = value.astype(jnp.bfloat16)
    low = (value - high.astype(jnp.float32)).astype(jnp.bfloat16)
    return high, low


def kernel(
    amp, vt, occ_s, occ_v, lab, out,
    land, lhs, rhs, part, core_in, own, from_left, from_right, to_right, to_left,
    final, sib, gsend, grecv, gsib,
    a2a_s, a2a_r, loc, core_s, core_r, right_s, right_r, left_s, left_r, sib_s, sib_r, g_s, g_r, gs_s, gs_r,
):
    a, c = lax.axis_index("row"), lax.axis_index("col")
    z, core = lax.div(c, 2), lax.rem(c, 2)
    other = 1 - core
    sibling = (a, 2 * z + other)
    a_hi, a_lo = lax.div(a, 2), lax.rem(a, 2)
    peers = [a, 2 * a_hi + 1 - a_lo, 2 * (1 - a_hi) + a_lo, 2 * (1 - a_hi) + 1 - a_lo]
    flips = [None, a_lo, a_hi, a_hi]

    def flip(h, s):
        return s if h == 0 else 1 - s

    def octet(index):
        return pl.ds(pl.multiple_of(8 * index, 8), 8)

    barrier = pltpu.get_barrier_semaphore()
    pl.semaphore_signal(barrier, 1, device_id=sibling, device_id_type=MESH)
    for t in (1, 2, 3):
        pl.semaphore_signal(barrier, 1, device_id=(peers[t], c), device_id_type=MESH)

    @pl.when(z > 0)
    def _():
        pl.semaphore_signal(barrier, 1, device_id=(a, c - 2), device_id_type=MESH)

    @pl.when(z < 3)
    def _():
        pl.semaphore_signal(barrier, 1, device_id=(a, c + 2), device_id_type=MESH)

    @pl.when((z == 0) | (z == 3))
    def _():
        pl.semaphore_wait(barrier, 5)

    @pl.when((z == 1) | (z == 2))
    def _():
        pl.semaphore_wait(barrier, 6)

    exchanged = {}
    for t in (3, 1, 2):
        for h in (0, 1):
            n = 2 * (t - 1) + h
            theirs = 1 - flips[t]
            copy = pltpu.make_async_remote_copy(
                src_ref=amp.at[octet(flip(h, theirs)), octet(2 * peers[t] + h), :],
                dst_ref=land.at[n], send_sem=a2a_s.at[n], recv_sem=a2a_r.at[n],
                device_id=(peers[t], c), device_id_type=MESH,
            )
            copy.start()
            exchanged[n] = copy
    local = {}
    for n, (first, second) in ((6, (0, 0)), (7, (1, 1)), (8, (1, 0))):
        copy = pltpu.make_async_copy(
            amp.at[8 * first:8 * first + 8, octet(2 * a + second), :], land.at[n], loc.at[n - 6]
        )
        copy.start()
        local[n] = copy

    depth = vt.shape[1]
    v_high, v_low = split(vt[...])
    rhs[:, 0:depth] = v_high
    rhs[:, depth:2 * depth] = v_low
    rhs[:, 2 * depth:3 * depth] = v_high
    labels = lab[...]
    core_copies = {}

    def fill(n, base):
        if n < 6:
            t, h = n // 2 + 1, n % 2
            exchanged[n].wait_recv()
            own_oct, col = h, 2 * peers[t] + flip(h, flips[t])
        else:
            local[n].wait()
            own_oct = 0 if n == 8 else n - 6
            col = 2 * a + (1 if n == 8 else n - 6)
        column_sym = occ_v[octet(col), :]
        for i in range(8):
            row = 8 * own_oct + i
            pair_sym = jnp.bitwise_xor(column_sym, occ_s[16 * a + row])
            total = amp[row, octet(col), :] + land[n, :, i, :]
            total = jnp.where(pair_sym == labels, total, jnp.float32(0.0))
            high, low = split(total)
            lhs[base + 8 * i:base + 8 * i + 8, 0:depth] = high.astype(jnp.float32)
            lhs[base + 8 * i:base + 8 * i + 8, depth:2 * depth] = low.astype(jnp.float32)

    def multiply(group):
        rows = 64 * len(group)
        for slot, n in enumerate(group):
            fill(n, 64 * slot)
        high = lhs[0:rows, 0:depth].astype(jnp.bfloat16)
        low = lhs[0:rows, depth:2 * depth].astype(jnp.bfloat16)
        stacked = jnp.concatenate([high, high, low], axis=1)
        product = lax.dot_general(
            stacked, rhs[...], (((1,), (1,)), ((), ())), preferred_element_type=jnp.float32
        )
        for slot, n in enumerate(group):
            part[n] = product[64 * slot:64 * slot + 64].reshape(8, 8, product.shape[1])
            copy = pltpu.make_async_remote_copy(
                src_ref=part.at[n, pl.ds(4 * other, 4)], dst_ref=core_in.at[n],
                send_sem=core_s.at[n], recv_sem=core_r.at[n], device_id=sibling, device_id_type=MESH,
            )
            copy.start()
            core_copies[n] = copy

    groups = ((6, 7, 8), (4, 5, 0, 1), (2, 3))
    order = sum(groups, ())

    def chain(n, source, sems, target):
        return pltpu.make_async_remote_copy(
            src_ref=source.at[n], dst_ref=(from_left if sems == "right" else from_right).at[n],
            send_sem=(right_s if sems == "right" else left_s).at[n],
            recv_sem=(right_r if sems == "right" else left_r).at[n],
            device_id=target, device_id_type=MESH,
        )

    def right(n, source):
        return chain(n, source, "right", (a, lax.rem(c + 2, 8)))

    def left(n, source):
        return chain(n, source, "left", (a, lax.rem(c + 6, 8)))

    def gather(n):
        core_copies[n].wait_recv()
        own[n] = part[n, pl.ds(4 * core, 4)] + core_in[n]

        @pl.when(z == 0)
        def _():
            right(n, own).start()

        @pl.when(z == 3)
        def _():
            left(n, own).start()

    for group in groups:
        multiply(group)
        for n in group:
            gather(n)

    def pass_right(n):
        right(n, to_right).wait_recv()
        to_right[n] = own[n] + from_left[n]
        right(n, to_right).start()

    def pass_left(n):
        left(n, to_left).wait_recv()
        to_left[n] = own[n] + from_right[n]
        left(n, to_left).start()

    lag = 2

    @pl.when(z == 0)
    def _():
        for n in order:
            left(n, own).wait_recv()
            final[n] = own[n] + from_right[n]
        for n in order:
            right(n, own).wait_send()

    @pl.when(z == 3)
    def _():
        for n in order:
            right(n, own).wait_recv()
            final[n] = own[n] + from_left[n]
        for n in order:
            left(n, own).wait_send()

    @pl.when(z == 1)
    def _():
        for q in range(BLOCKS + lag):
            if q < BLOCKS:
                pass_right(order[q])
            if q >= lag:
                n = order[q - lag]
                pass_left(n)
                final[n] = to_right[n] + from_right[n]
        for n in order:
            right(n, to_right).wait_send()
            left(n, to_left).wait_send()

    @pl.when(z == 2)
    def _():
        for q in range(BLOCKS + lag):
            if q < BLOCKS:
                pass_left(order[q])
            if q >= lag:
                n = order[q - lag]
                pass_right(n)
                final[n] = to_left[n] + from_left[n]
        for n in order:
            right(n, to_right).wait_send()
            left(n, to_left).wait_send()

    half, odd = lax.div(z, 2), lax.rem(z, 2)
    ends = []
    g_copies = {}
    for t in (3, 1, 2):
        s = flips[t]
        h = half + s - 2 * half * s
        value = final[2 * (t - 1) + h]
        for q in range(2):
            rows = [
                jnp.where(odd == 1, value[2 * q + e, 4:8, :], value[2 * q + e, 0:4, :]) for e in (0, 1)
            ]
            gsend[t - 1, q] = jnp.concatenate(rows, axis=0)
        copy = pltpu.make_async_remote_copy(
            src_ref=gsend.at[t - 1], dst_ref=grecv.at[t - 1], send_sem=g_s.at[t - 1],
            recv_sem=g_r.at[t - 1], device_id=(peers[t], c), device_id_type=MESH,
        )
        copy.start()
        g_copies[t] = copy
    for slot in range(5):
        index = (2 * slot + half) if slot < 4 else 8
        copy = pltpu.make_async_remote_copy(
            src_ref=final.at[index], dst_ref=sib.at[slot], send_sem=sib_s.at[slot],
            recv_sem=sib_r.at[slot], device_id=sibling, device_id_type=MESH,
        )
        copy.start()
        ends.append(copy)
    for copy in ends:
        copy.wait_recv()

    def direct(slot, il):
        mine = final[(2 * slot + half) if slot < 4 else 8, 2 * core + il]
        theirs = sib[slot, 2 * core + il]
        return jnp.where(odd == core, mine, theirs)

    for il in range(2):
        for t in (1, 2, 3):
            s = flips[t]
            out[il, octet(2 * peers[t] + (half + s - 2 * half * s)), :] = direct(t - 1, il)
        out[il, octet(2 * a + half), :] = direct(3, il)
        straight = direct(4, il)
        rows = []
        for j in range(8):
            def pick(ref_row):
                options = [ref_row[4 * o + 2 * k + il:4 * o + 2 * k + il + 1, :] for o in (0, 1) for k in (0, 1)]
                even = jnp.where(core == 1, options[1], options[0])
                uneven = jnp.where(core == 1, options[3], options[2])
                return jnp.where(odd == 1, uneven, even)
            mine, theirs = pick(final[8, j % 4]), pick(sib[4, j % 4])
            rows.append(jnp.where(core == j // 4, mine, theirs))
        turned = jnp.concatenate(rows, axis=0)
        out[il, octet(2 * a + 1 - half), :] = jnp.where(half == 0, straight, turned)

    g_sib = {}
    for t in (3, 1, 2):
        g_copies[t].wait_recv()
        copy = pltpu.make_async_remote_copy(
            src_ref=grecv.at[t - 1], dst_ref=gsib.at[t - 1], send_sem=gs_s.at[t - 1],
            recv_sem=gs_r.at[t - 1], device_id=sibling, device_id_type=MESH,
        )
        copy.start()
        g_sib[t] = copy
    for t in (3, 1, 2):
        g_sib[t].wait_recv()
        s = flips[t]
        g = 1 - (half + s - 2 * half * s)
        for il in range(2):
            rows = []
            for j in range(8):
                q, e = (j % 4) // 2, j % 2

                def pick(tile):
                    low = tile[4 * e + il:4 * e + il + 1, :]
                    high = tile[4 * e + 2 + il:4 * e + 3 + il, :]
                    return jnp.where(core == 1, high, low)
                mine, theirs = pick(grecv[t - 1, q]), pick(gsib[t - 1, q])
                rows.append(jnp.where(core == j // 4, mine, theirs))
            out[il, octet(2 * peers[t] + g), :] = jnp.concatenate(rows, axis=0)

    for n in range(6):
        exchanged[n].wait_send()
    for n in range(BLOCKS):
        core_copies[n].wait_send()
    for copy in ends:
        copy.wait_send()
    for t in (1, 2, 3):
        g_copies[t].wait_send()
        g_sib[t].wait_send()


def paired_body(amplitudes, integrals, occ_irrep, cd_irrep):
    depth, width = integrals.shape
    vmem = pl.BlockSpec(memory_space=pltpu.VMEM)
    smem = pl.BlockSpec(memory_space=pltpu.SMEM)
    f32 = jnp.float32

    def sums(count):
        return pltpu.VMEM((count, 4, 8, width), f32)

    def sems(count):
        return [pltpu.SemaphoreType.DMA((count,))] * 2

    result = pl.pallas_call(
        kernel,
        out_shape=jax.ShapeDtypeStruct((2, 64, width), f32),
        in_specs=[vmem, vmem, smem, vmem, vmem],
        out_specs=vmem,
        scratch_shapes=[
            pltpu.VMEM((BLOCKS, 8, 8, depth), f32),
            pltpu.VMEM((256, 2 * depth), f32),
            pltpu.VMEM((width, 3 * depth), jnp.bfloat16),
            pltpu.VMEM((BLOCKS, 8, 8, width), f32),
            sums(BLOCKS), sums(BLOCKS), sums(BLOCKS), sums(BLOCKS), sums(BLOCKS), sums(BLOCKS),
            sums(BLOCKS), sums(5),
            pltpu.VMEM((3, 2, 8, width), f32),
            pltpu.VMEM((3, 2, 8, width), f32),
            pltpu.VMEM((3, 2, 8, width), f32),
            *sems(6), pltpu.SemaphoreType.DMA((3,)),
            *sems(BLOCKS), *sems(BLOCKS), *sems(BLOCKS), *sems(5), *sems(3), *sems(3),
        ],
        compiler_params=pltpu.CompilerParams(
            collective_id=0, has_side_effects=True, vmem_limit_bytes=50 << 20
        ),
    )(amplitudes, integrals.T, occ_irrep, occ_irrep.reshape(64, 1), cd_irrep.reshape(1, depth))
    return result.reshape(128, width)


def solution(mesh):
    in_specs = (P("row", None, "col"), P("col", None), P(), P("col"))
    out_specs = P(("row", "col"), None)
    fits = mesh.shape["row"] == 4 and mesh.shape["col"] == 8

    def body(amplitudes, integrals, occ_irrep, cd_irrep):
        paired = fits and amplitudes.shape[:2] == (16, 64)
        chosen = paired_body if paired else plain_body
        return chosen(amplitudes, integrals, occ_irrep, cd_irrep)

    return jax.shard_map(body, mesh=mesh, in_specs=in_specs, out_specs=out_specs, check_vma=False)
```

```python
import jax
import jax.numpy as jnp
from jax import lax
from jax.experimental import pallas as pl
from jax.experimental.pallas import tpu as pltpu
from jax.sharding import PartitionSpec as P

MESH = pl.DeviceIdType.MESH
BLOCKS = 9


def plain_body(amplitudes, integrals, occ_irrep, cd_irrep):
    own_count = amplitudes.shape[0]
    occupied = amplitudes.shape[1]
    received = lax.all_to_all(amplitudes, "row", split_axis=1, concat_axis=0, tiled=True)
    mirrored = jnp.swapaxes(received, 0, 1)
    first_i = lax.axis_index("row") * own_count
    own_irrep = lax.dynamic_slice_in_dim(occ_irrep, first_i, own_count, 0)
    pair_sym = jnp.bitwise_xor(own_irrep[:, None], occ_irrep[None, :])
    allowed = pair_sym[:, :, None] == cd_irrep[None, None, :]
    combined = jnp.where(allowed, amplitudes + mirrored, jnp.float32(0.0))
    combined = combined.reshape(own_count * occupied, amplitudes.shape[2])
    partial_value = jnp.dot(
        combined, integrals, precision=lax.Precision.HIGHEST, preferred_element_type=jnp.float32
    )
    return lax.psum_scatter(partial_value, "col", scatter_dimension=0, tiled=True)


def split(value):
    high = value.astype(jnp.bfloat16)
    low = (value - high.astype(jnp.float32)).astype(jnp.bfloat16)
    return high, low


def kernel(
    amp_hbm, vt_hbm, occ_s, lab, out,
    amp, vt, in_sem, land, lhs, rhs, part, core_in, own, from_left, from_right, to_right, to_left,
    final, sib, gsend, grecv, gsib,
    a2a_s, a2a_r, loc, core_s, core_r, right_s, right_r, left_s, left_r, sib_s, sib_r, g_s, g_r, gs_s, gs_r,
):
    a, c = lax.axis_index("row"), lax.axis_index("col")
    z, core = lax.div(c, 2), lax.rem(c, 2)
    other = 1 - core
    sibling = (a, 2 * z + other)
    a_hi, a_lo = lax.div(a, 2), lax.rem(a, 2)
    peers = [a, 2 * a_hi + 1 - a_lo, 2 * (1 - a_hi) + a_lo, 2 * (1 - a_hi) + 1 - a_lo]
    flips = [None, a_lo, a_hi, a_hi]

    def flip(h, s):
        return s if h == 0 else 1 - s

    def octet(index):
        return pl.ds(pl.multiple_of(8 * index, 8), 8)

    amp_copy = pltpu.make_async_copy(amp_hbm, amp, in_sem.at[0])
    vt_copy = pltpu.make_async_copy(vt_hbm, vt, in_sem.at[1])
    vt_copy.start()
    amp_copy.start()
    barrier = pltpu.get_barrier_semaphore()
    pl.semaphore_signal(barrier, 1, device_id=sibling, device_id_type=MESH)
    for t in (1, 2, 3):
        pl.semaphore_signal(barrier, 1, device_id=(peers[t], c), device_id_type=MESH)

    @pl.when(z > 0)
    def _():
        pl.semaphore_signal(barrier, 1, device_id=(a, c - 2), device_id_type=MESH)

    @pl.when(z < 3)
    def _():
        pl.semaphore_signal(barrier, 1, device_id=(a, c + 2), device_id_type=MESH)

    @pl.when((z == 0) | (z == 3))
    def _():
        pl.semaphore_wait(barrier, 5)

    @pl.when((z == 1) | (z == 2))
    def _():
        pl.semaphore_wait(barrier, 6)

    exchanged = {}
    for t in (3, 1, 2):
        for h in (0, 1):
            n = 2 * (t - 1) + h
            theirs = 1 - flips[t]
            copy = pltpu.make_async_remote_copy(
                src_ref=amp_hbm.at[octet(flip(h, theirs)), octet(2 * peers[t] + h), :],
                dst_ref=land.at[n], send_sem=a2a_s.at[n], recv_sem=a2a_r.at[n],
                device_id=(peers[t], c), device_id_type=MESH,
            )
            copy.start()
            exchanged[n] = copy
    local = {}
    for n, (first, second) in ((6, (0, 0)), (7, (1, 1)), (8, (1, 0))):
        copy = pltpu.make_async_copy(
            amp_hbm.at[8 * first:8 * first + 8, octet(2 * a + second), :], land.at[n], loc.at[n - 6]
        )
        copy.start()
        local[n] = copy

    width, depth = vt.shape
    full = width // 128
    rest = width % 128

    def unpack(packed, i):
        tiles = [packed[full * i + lane] for lane in range(full)]
        return jnp.concatenate(tiles + [packed[4 * full][:, rest * i:rest * i + rest]], axis=1)

    half, odd = lax.div(z, 2), lax.rem(z, 2)
    vt_copy.wait()
    v_high, v_low = split(vt[...])
    rhs[:, 0:depth] = v_high
    rhs[:, depth:2 * depth] = v_low
    rhs[:, 2 * depth:3 * depth] = v_high
    amp_copy.wait()
    labels = lab[...].reshape(1, depth)
    sublane = lax.broadcasted_iota(jnp.int32, (8, depth), 0)
    core_copies = {}

    def fill(n, base):
        if n < 6:
            t, h = n // 2 + 1, n % 2
            exchanged[n].wait_recv()
            own_oct, col = h, 2 * peers[t] + flip(h, flips[t])
        else:
            local[n].wait()
            own_oct = 0 if n == 8 else n - 6
            col = 2 * a + (1 if n == 8 else n - 6)
        column_sym = jnp.zeros((8, depth), jnp.int32)
        for j in range(8):
            column_sym = jnp.where(sublane == j, occ_s[8 * col + j], column_sym)
        column_sym = jnp.bitwise_xor(column_sym, labels)
        for i in range(8):
            row = 8 * own_oct + i
            total = amp[row, octet(col), :] + land[n, :, i, :]
            total = jnp.where(column_sym == occ_s[16 * a + row], total, jnp.float32(0.0))
            high, low = split(total)
            lhs[base + 8 * i:base + 8 * i + 8, 0:depth] = high.astype(jnp.float32)
            lhs[base + 8 * i:base + 8 * i + 8, depth:2 * depth] = low.astype(jnp.float32)

    def multiply(group):
        rows = 64 * len(group)
        for slot, n in enumerate(group):
            fill(n, 64 * slot)
        high = lhs[0:rows, 0:depth].astype(jnp.bfloat16)
        low = lhs[0:rows, depth:2 * depth].astype(jnp.bfloat16)
        stacked = jnp.concatenate([high, high, low], axis=1)
        product = lax.dot_general(
            stacked, rhs[...], (((1,), (1,)), ((), ())), preferred_element_type=jnp.float32
        )
        for slot, n in enumerate(group):
            for k in range(2):
                rows_of = [product[64 * slot + 32 * k + 8 * i:64 * slot + 32 * k + 8 * i + 8] for i in range(4)]
                for i in range(4):
                    for lane in range(full):
                        part[n, k, full * i + lane] = rows_of[i][:, 128 * lane:128 * lane + 128]
                part[n, k, 4 * full] = jnp.concatenate([r[:, 128 * full:] for r in rows_of], axis=1)
            copy = pltpu.make_async_remote_copy(
                src_ref=part.at[n, other], dst_ref=core_in.at[n],
                send_sem=core_s.at[n], recv_sem=core_r.at[n], device_id=sibling, device_id_type=MESH,
            )
            copy.start()
            core_copies[n] = copy

    groups = ((6, 7, 8), (4, 5, 0, 1), (2, 3))
    order = sum(groups, ())

    def chain(n, source, sems, target):
        return pltpu.make_async_remote_copy(
            src_ref=source.at[n], dst_ref=(from_left if sems == "right" else from_right).at[n],
            send_sem=(right_s if sems == "right" else left_s).at[n],
            recv_sem=(right_r if sems == "right" else left_r).at[n],
            device_id=target, device_id_type=MESH,
        )

    def right(n, source):
        return chain(n, source, "right", (a, lax.rem(c + 2, 8)))

    def left(n, source):
        return chain(n, source, "left", (a, lax.rem(c + 6, 8)))

    def gather(n):
        core_copies[n].wait_recv()
        own[n] = part[n, core] + core_in[n]

        @pl.when(z == 0)
        def _():
            right(n, own).start()

        @pl.when(z == 3)
        def _():
            left(n, own).start()

    for group in groups:
        multiply(group)
        for n in group:
            gather(n)

    def g_copy(t):
        return pltpu.make_async_remote_copy(
            src_ref=gsend.at[t - 1], dst_ref=grecv.at[t - 1], send_sem=g_s.at[t - 1],
            recv_sem=g_r.at[t - 1], device_id=(peers[t], c), device_id_type=MESH,
        )

    def sib_copy(slot):
        return pltpu.make_async_remote_copy(
            src_ref=final.at[(2 * slot + half) if slot < 4 else 8], dst_ref=sib.at[slot],
            send_sem=sib_s.at[slot], recv_sem=sib_r.at[slot], device_id=sibling, device_id_type=MESH,
        )

    def finish(n):
        if n in (1, 3, 5):
            t = n // 2 + 1
            s = flips[t]
            value = final[2 * (t - 1) + (half + s - 2 * half * s)]
            for q in range(2):
                pair = [unpack(value, 2 * q + e) for e in (0, 1)]
                rows = [jnp.where(odd == 1, p[4:8, :], p[0:4, :]) for p in pair]
                gsend[t - 1, q] = jnp.concatenate(rows, axis=0)
            g_copy(t).start()
        if n in (1, 3, 5, 7, 8):
            sib_copy(n // 2).start()

    def pass_right(n):
        right(n, to_right).wait_recv()
        to_right[n] = own[n] + from_left[n]
        right(n, to_right).start()

    def pass_left(n):
        left(n, to_left).wait_recv()
        to_left[n] = own[n] + from_right[n]
        left(n, to_left).start()

    lag = 2

    @pl.when(z == 0)
    def _():
        for n in order:
            left(n, own).wait_recv()
            final[n] = own[n] + from_right[n]
            finish(n)
        for n in order:
            right(n, own).wait_send()

    @pl.when(z == 3)
    def _():
        for n in order:
            right(n, own).wait_recv()
            final[n] = own[n] + from_left[n]
            finish(n)
        for n in order:
            left(n, own).wait_send()

    @pl.when(z == 1)
    def _():
        for q in range(BLOCKS + lag):
            if q < BLOCKS:
                pass_right(order[q])
            if q >= lag:
                n = order[q - lag]
                pass_left(n)
                final[n] = to_right[n] + from_right[n]
                finish(n)
        for n in order:
            right(n, to_right).wait_send()
            left(n, to_left).wait_send()

    @pl.when(z == 2)
    def _():
        for q in range(BLOCKS + lag):
            if q < BLOCKS:
                pass_left(order[q])
            if q >= lag:
                n = order[q - lag]
                pass_right(n)
                final[n] = to_left[n] + from_left[n]
                finish(n)
        for n in order:
            right(n, to_right).wait_send()
            left(n, to_left).wait_send()

    g_copies = {t: g_copy(t) for t in (3, 1, 2)}
    ends = [sib_copy(slot) for slot in range(5)]
    for copy in ends:
        copy.wait_recv()

    def direct(slot, il):
        mine = final[(2 * slot + half) if slot < 4 else 8]
        chosen = jnp.where(odd == core, mine, sib[slot])
        return jnp.where(core == 1, unpack(chosen, 2 + il), unpack(chosen, il))

    for il in range(2):
        for t in (1, 2, 3):
            s = flips[t]
            out[il, octet(2 * peers[t] + (half + s - 2 * half * s)), :] = direct(t - 1, il)
        out[il, octet(2 * a + half), :] = direct(3, il)
        straight = direct(4, il)
        rows = []
        mine_all, theirs_all = final[8], sib[4]
        for j in range(8):
            def pick(ref_row):
                options = [ref_row[4 * o + 2 * k + il:4 * o + 2 * k + il + 1, :] for o in (0, 1) for k in (0, 1)]
                even = jnp.where(core == 1, options[1], options[0])
                uneven = jnp.where(core == 1, options[3], options[2])
                return jnp.where(odd == 1, uneven, even)
            mine, theirs = pick(unpack(mine_all, j % 4)), pick(unpack(theirs_all, j % 4))
            rows.append(jnp.where(core == j // 4, mine, theirs))
        turned = jnp.concatenate(rows, axis=0)
        out[il, octet(2 * a + 1 - half), :] = jnp.where(half == 0, straight, turned)

    g_sib = {}
    for t in (3, 1, 2):
        g_copies[t].wait_recv()
        copy = pltpu.make_async_remote_copy(
            src_ref=grecv.at[t - 1], dst_ref=gsib.at[t - 1], send_sem=gs_s.at[t - 1],
            recv_sem=gs_r.at[t - 1], device_id=sibling, device_id_type=MESH,
        )
        copy.start()
        g_sib[t] = copy
    for t in (3, 1, 2):
        g_sib[t].wait_recv()
        s = flips[t]
        g = 1 - (half + s - 2 * half * s)
        for il in range(2):
            rows = []
            for j in range(8):
                q, e = (j % 4) // 2, j % 2

                def pick(tile):
                    low = tile[4 * e + il:4 * e + il + 1, :]
                    high = tile[4 * e + 2 + il:4 * e + 3 + il, :]
                    return jnp.where(core == 1, high, low)
                mine, theirs = pick(grecv[t - 1, q]), pick(gsib[t - 1, q])
                rows.append(jnp.where(core == j // 4, mine, theirs))
            out[il, octet(2 * peers[t] + g), :] = jnp.concatenate(rows, axis=0)

    for n in range(6):
        exchanged[n].wait_send()
    for n in range(BLOCKS):
        core_copies[n].wait_send()
    for copy in ends:
        copy.wait_send()
    for t in (1, 2, 3):
        g_copies[t].wait_send()
        g_sib[t].wait_send()


def paired_body(amplitudes, integrals, occ_irrep, cd_irrep):
    depth, width = integrals.shape
    vmem = pl.BlockSpec(memory_space=pltpu.VMEM)
    hbm = pl.BlockSpec(memory_space=pl.ANY)
    smem = pl.BlockSpec(memory_space=pltpu.SMEM)
    f32 = jnp.float32
    tiles = 4 * (width // 128) + 1

    def sums(count):
        return pltpu.VMEM((count, tiles, 8, 128), f32)

    def sems(count):
        return [pltpu.SemaphoreType.DMA((count,))] * 2

    result = pl.pallas_call(
        kernel,
        out_shape=jax.ShapeDtypeStruct((2, 64, width), f32),
        in_specs=[hbm, hbm, smem, vmem],
        out_specs=vmem,
        scratch_shapes=[
            pltpu.VMEM(amplitudes.shape, f32),
            pltpu.VMEM((width, depth), f32),
            pltpu.SemaphoreType.DMA((2,)),
            pltpu.VMEM((BLOCKS, 8, 8, depth), f32),
            pltpu.VMEM((256, 2 * depth), f32),
            pltpu.VMEM((width, 3 * depth), jnp.bfloat16),
            pltpu.VMEM((BLOCKS, 2, tiles, 8, 128), f32),
            sums(BLOCKS), sums(BLOCKS), sums(BLOCKS), sums(BLOCKS), sums(BLOCKS), sums(BLOCKS),
            sums(BLOCKS), sums(5),
            pltpu.VMEM((3, 2, 8, width), f32),
            pltpu.VMEM((3, 2, 8, width), f32),
            pltpu.VMEM((3, 2, 8, width), f32),
            *sems(6), pltpu.SemaphoreType.DMA((3,)),
            *sems(BLOCKS), *sems(BLOCKS), *sems(BLOCKS), *sems(5), *sems(3), *sems(3),
        ],
        compiler_params=pltpu.CompilerParams(
            collective_id=0, has_side_effects=True, vmem_limit_bytes=50 << 20
        ),
    )(amplitudes, integrals.T, occ_irrep, cd_irrep)
    return result.reshape(128, width)


def solution(mesh):
    in_specs = (P("row", None, "col"), P("col", None), P(), P("col"))
    out_specs = P(("row", "col"), None)
    fits = mesh.shape["row"] == 4 and mesh.shape["col"] == 8

    def body(amplitudes, integrals, occ_irrep, cd_irrep):
        paired = fits and amplitudes.shape[:2] == (16, 64) and integrals.shape[1] % 128 == 32
        chosen = paired_body if paired else plain_body
        return chosen(amplitudes, integrals, occ_irrep, cd_irrep)

    return jax.shard_map(body, mesh=mesh, in_specs=in_specs, out_specs=out_specs, check_vma=False)
```

```python
import jax
import jax.numpy as jnp
from jax import lax
from jax.experimental import pallas as pl
from jax.experimental.pallas import tpu as pltpu
from jax.sharding import PartitionSpec as P

MESH = pl.DeviceIdType.MESH
BLOCKS = 9


def plain_body(amplitudes, integrals, occ_irrep, cd_irrep):
    own_count = amplitudes.shape[0]
    occupied = amplitudes.shape[1]
    received = lax.all_to_all(amplitudes, "row", split_axis=1, concat_axis=0, tiled=True)
    mirrored = jnp.swapaxes(received, 0, 1)
    first_i = lax.axis_index("row") * own_count
    own_irrep = lax.dynamic_slice_in_dim(occ_irrep, first_i, own_count, 0)
    pair_sym = jnp.bitwise_xor(own_irrep[:, None], occ_irrep[None, :])
    allowed = pair_sym[:, :, None] == cd_irrep[None, None, :]
    combined = jnp.where(allowed, amplitudes + mirrored, jnp.float32(0.0))
    combined = combined.reshape(own_count * occupied, amplitudes.shape[2])
    partial_value = jnp.dot(
        combined, integrals, precision=lax.Precision.HIGHEST, preferred_element_type=jnp.float32
    )
    return lax.psum_scatter(partial_value, "col", scatter_dimension=0, tiled=True)


def split(value):
    high = value.astype(jnp.bfloat16)
    low = (value - high.astype(jnp.float32)).astype(jnp.bfloat16)
    return high, low


def kernel(
    amp_hbm, vt_hbm, occ_s, lab, out,
    amp, vt, in_sem, land, lhs, rhs, part, core_in, own, from_left, from_right, to_right, to_left,
    final, sib, gsend, grecv, gsib,
    a2a_s, a2a_r, loc, core_s, core_r, right_s, right_r, left_s, left_r, sib_s, sib_r, g_s, g_r, gs_s, gs_r,
):
    a, c = lax.axis_index("row"), lax.axis_index("col")
    z, core = lax.div(c, 2), lax.rem(c, 2)
    other = 1 - core
    sibling = (a, 2 * z + other)
    a_hi, a_lo = lax.div(a, 2), lax.rem(a, 2)
    peers = [a, 2 * a_hi + 1 - a_lo, 2 * (1 - a_hi) + a_lo, 2 * (1 - a_hi) + 1 - a_lo]
    flips = [None, a_lo, a_hi, a_hi]

    def flip(h, s):
        return s if h == 0 else 1 - s

    def octet(index):
        return pl.ds(pl.multiple_of(8 * index, 8), 8)

    amp_copy = pltpu.make_async_copy(amp_hbm, amp, in_sem.at[0])
    vt_copy = pltpu.make_async_copy(vt_hbm, vt, in_sem.at[1])
    vt_copy.start()
    amp_copy.start()
    barrier = pltpu.get_barrier_semaphore()
    pl.semaphore_signal(barrier, 1, device_id=sibling, device_id_type=MESH)
    for t in (1, 2, 3):
        pl.semaphore_signal(barrier, 1, device_id=(peers[t], c), device_id_type=MESH)

    @pl.when(z > 0)
    def _():
        pl.semaphore_signal(barrier, 1, device_id=(a, c - 2), device_id_type=MESH)

    @pl.when(z < 3)
    def _():
        pl.semaphore_signal(barrier, 1, device_id=(a, c + 2), device_id_type=MESH)

    @pl.when((z == 0) | (z == 3))
    def _():
        pl.semaphore_wait(barrier, 5)

    @pl.when((z == 1) | (z == 2))
    def _():
        pl.semaphore_wait(barrier, 6)

    exchanged = {}
    for t in (3, 1, 2):
        for h in (0, 1):
            n = 2 * (t - 1) + h
            theirs = 1 - flips[t]
            copy = pltpu.make_async_remote_copy(
                src_ref=amp_hbm.at[octet(flip(h, theirs)), octet(2 * peers[t] + h), :],
                dst_ref=land.at[n], send_sem=a2a_s.at[n], recv_sem=a2a_r.at[n],
                device_id=(peers[t], c), device_id_type=MESH,
            )
            copy.start()
            exchanged[n] = copy
    local = {}
    for n, (first, second) in ((6, (0, 0)), (7, (1, 1)), (8, (1, 0))):
        copy = pltpu.make_async_copy(
            amp_hbm.at[8 * first:8 * first + 8, octet(2 * a + second), :], land.at[n], loc.at[n - 6]
        )
        copy.start()
        local[n] = copy

    width, depth = vt.shape
    full = width // 128
    rest = width % 128

    def unpack(packed, i):
        tiles = [packed[full * i + lane] for lane in range(full)]
        return jnp.concatenate(tiles + [packed[4 * full][:, rest * i:rest * i + rest]], axis=1)

    half, odd = lax.div(z, 2), lax.rem(z, 2)
    vt_copy.wait()
    v_high, v_low = split(vt[...])
    rhs[:, 0:depth] = v_high
    rhs[:, depth:2 * depth] = v_low
    rhs[:, 2 * depth:3 * depth] = v_high
    amp_copy.wait()
    labels = lab[...].reshape(1, depth)
    sublane = lax.broadcasted_iota(jnp.int32, (8, depth), 0)
    core_copies = {}

    def fill(n, base):
        if n < 6:
            t, h = n // 2 + 1, n % 2
            exchanged[n].wait_recv()
            own_oct, col = h, 2 * peers[t] + flip(h, flips[t])
        else:
            local[n].wait()
            own_oct = 0 if n == 8 else n - 6
            col = 2 * a + (1 if n == 8 else n - 6)
        column_sym = jnp.zeros((8, depth), jnp.int32)
        for j in range(8):
            column_sym = jnp.where(sublane == j, occ_s[8 * col + j], column_sym)
        column_sym = jnp.bitwise_xor(column_sym, labels)
        for i in range(8):
            row = 8 * own_oct + i
            total = amp[row, octet(col), :] + land[n, :, i, :]
            total = jnp.where(column_sym == occ_s[16 * a + row], total, jnp.float32(0.0))
            high, low = split(total)
            lhs[base + 8 * i:base + 8 * i + 8, 0:depth] = high.astype(jnp.float32)
            lhs[base + 8 * i:base + 8 * i + 8, depth:2 * depth] = low.astype(jnp.float32)

    def multiply(group):
        rows = 64 * len(group)
        for slot, n in enumerate(group):
            fill(n, 64 * slot)
        high = lhs[0:rows, 0:depth].astype(jnp.bfloat16)
        low = lhs[0:rows, depth:2 * depth].astype(jnp.bfloat16)
        stacked = jnp.concatenate([high, high, low], axis=1)
        product = lax.dot_general(
            stacked, rhs[...], (((1,), (1,)), ((), ())), preferred_element_type=jnp.float32
        )
        for slot, n in enumerate(group):
            for k in range(2):
                rows_of = [product[64 * slot + 32 * k + 8 * i:64 * slot + 32 * k + 8 * i + 8] for i in range(4)]
                for i in range(4):
                    for lane in range(full):
                        part[n, k, full * i + lane] = rows_of[i][:, 128 * lane:128 * lane + 128]
                part[n, k, 4 * full] = jnp.concatenate([r[:, 128 * full:] for r in rows_of], axis=1)
            copy = pltpu.make_async_remote_copy(
                src_ref=part.at[n, other], dst_ref=core_in.at[n],
                send_sem=core_s.at[n], recv_sem=core_r.at[n], device_id=sibling, device_id_type=MESH,
            )
            copy.start()
            core_copies[n] = copy

    groups = ((6, 7, 8), (4, 5), (0, 1), (2, 3))
    order = sum(groups, ())

    def chain(n, source, sems, target):
        return pltpu.make_async_remote_copy(
            src_ref=source.at[n], dst_ref=(from_left if sems == "right" else from_right).at[n],
            send_sem=(right_s if sems == "right" else left_s).at[n],
            recv_sem=(right_r if sems == "right" else left_r).at[n],
            device_id=target, device_id_type=MESH,
        )

    def right(n, source):
        return chain(n, source, "right", (a, lax.rem(c + 2, 8)))

    def left(n, source):
        return chain(n, source, "left", (a, lax.rem(c + 6, 8)))

    def gather(n):
        core_copies[n].wait_recv()
        own[n] = part[n, core] + core_in[n]

        @pl.when(z == 0)
        def _():
            right(n, own).start()

        @pl.when(z == 3)
        def _():
            left(n, own).start()

    for group in groups:
        multiply(group)
        for n in group:
            gather(n)

    def g_copy(t):
        return pltpu.make_async_remote_copy(
            src_ref=gsend.at[t - 1], dst_ref=grecv.at[t - 1], send_sem=g_s.at[t - 1],
            recv_sem=g_r.at[t - 1], device_id=(peers[t], c), device_id_type=MESH,
        )

    def sib_copy(slot):
        return pltpu.make_async_remote_copy(
            src_ref=final.at[(2 * slot + half) if slot < 4 else 8], dst_ref=sib.at[slot],
            send_sem=sib_s.at[slot], recv_sem=sib_r.at[slot], device_id=sibling, device_id_type=MESH,
        )

    def finish(n):
        if n in (1, 3, 5):
            t = n // 2 + 1
            s = flips[t]
            value = final[2 * (t - 1) + (half + s - 2 * half * s)]
            for q in range(2):
                pair = [unpack(value, 2 * q + e) for e in (0, 1)]
                rows = [jnp.where(odd == 1, p[4:8, :], p[0:4, :]) for p in pair]
                gsend[t - 1, q] = jnp.concatenate(rows, axis=0)
            g_copy(t).start()
        if n in (1, 3, 5, 7, 8):
            sib_copy(n // 2).start()

    def pass_right(n):
        right(n, to_right).wait_recv()
        to_right[n] = own[n] + from_left[n]
        right(n, to_right).start()

    def pass_left(n):
        left(n, to_left).wait_recv()
        to_left[n] = own[n] + from_right[n]
        left(n, to_left).start()

    lag = 2

    @pl.when(z == 0)
    def _():
        for n in order:
            left(n, own).wait_recv()
            final[n] = own[n] + from_right[n]
            finish(n)
        for n in order:
            right(n, own).wait_send()

    @pl.when(z == 3)
    def _():
        for n in order:
            right(n, own).wait_recv()
            final[n] = own[n] + from_left[n]
            finish(n)
        for n in order:
            left(n, own).wait_send()

    @pl.when(z == 1)
    def _():
        for q in range(BLOCKS + lag):
            if q < BLOCKS:
                pass_right(order[q])
            if q >= lag:
                n = order[q - lag]
                pass_left(n)
                final[n] = to_right[n] + from_right[n]
                finish(n)
        for n in order:
            right(n, to_right).wait_send()
            left(n, to_left).wait_send()

    @pl.when(z == 2)
    def _():
        for q in range(BLOCKS + lag):
            if q < BLOCKS:
                pass_left(order[q])
            if q >= lag:
                n = order[q - lag]
                pass_right(n)
                final[n] = to_left[n] + from_left[n]
                finish(n)
        for n in order:
            right(n, to_right).wait_send()
            left(n, to_left).wait_send()

    g_copies = {t: g_copy(t) for t in (3, 1, 2)}
    ends = [sib_copy(slot) for slot in range(5)]
    for copy in ends:
        copy.wait_recv()

    def direct(slot, il):
        mine = final[(2 * slot + half) if slot < 4 else 8]
        chosen = jnp.where(odd == core, mine, sib[slot])
        return jnp.where(core == 1, unpack(chosen, 2 + il), unpack(chosen, il))

    for il in range(2):
        for t in (1, 2, 3):
            s = flips[t]
            out[il, octet(2 * peers[t] + (half + s - 2 * half * s)), :] = direct(t - 1, il)
        out[il, octet(2 * a + half), :] = direct(3, il)
        straight = direct(4, il)
        rows = []
        mine_all, theirs_all = final[8], sib[4]
        for j in range(8):
            def pick(ref_row):
                options = [ref_row[4 * o + 2 * k + il:4 * o + 2 * k + il + 1, :] for o in (0, 1) for k in (0, 1)]
                even = jnp.where(core == 1, options[1], options[0])
                uneven = jnp.where(core == 1, options[3], options[2])
                return jnp.where(odd == 1, uneven, even)
            mine, theirs = pick(unpack(mine_all, j % 4)), pick(unpack(theirs_all, j % 4))
            rows.append(jnp.where(core == j // 4, mine, theirs))
        turned = jnp.concatenate(rows, axis=0)
        out[il, octet(2 * a + 1 - half), :] = jnp.where(half == 0, straight, turned)

    g_sib = {}
    for t in (3, 1, 2):
        g_copies[t].wait_recv()
        copy = pltpu.make_async_remote_copy(
            src_ref=grecv.at[t - 1], dst_ref=gsib.at[t - 1], send_sem=gs_s.at[t - 1],
            recv_sem=gs_r.at[t - 1], device_id=sibling, device_id_type=MESH,
        )
        copy.start()
        g_sib[t] = copy
    for t in (3, 1, 2):
        g_sib[t].wait_recv()
        s = flips[t]
        g = 1 - (half + s - 2 * half * s)
        for il in range(2):
            rows = []
            for j in range(8):
                q, e = (j % 4) // 2, j % 2

                def pick(tile):
                    low = tile[4 * e + il:4 * e + il + 1, :]
                    high = tile[4 * e + 2 + il:4 * e + 3 + il, :]
                    return jnp.where(core == 1, high, low)
                mine, theirs = pick(grecv[t - 1, q]), pick(gsib[t - 1, q])
                rows.append(jnp.where(core == j // 4, mine, theirs))
            out[il, octet(2 * peers[t] + g), :] = jnp.concatenate(rows, axis=0)

    for n in range(6):
        exchanged[n].wait_send()
    for n in range(BLOCKS):
        core_copies[n].wait_send()
    for copy in ends:
        copy.wait_send()
    for t in (1, 2, 3):
        g_copies[t].wait_send()
        g_sib[t].wait_send()


def paired_body(amplitudes, integrals, occ_irrep, cd_irrep):
    depth, width = integrals.shape
    vmem = pl.BlockSpec(memory_space=pltpu.VMEM)
    hbm = pl.BlockSpec(memory_space=pl.ANY)
    smem = pl.BlockSpec(memory_space=pltpu.SMEM)
    f32 = jnp.float32
    tiles = 4 * (width // 128) + 1

    def sums(count):
        return pltpu.VMEM((count, tiles, 8, 128), f32)

    def sems(count):
        return [pltpu.SemaphoreType.DMA((count,))] * 2

    result = pl.pallas_call(
        kernel,
        out_shape=jax.ShapeDtypeStruct((2, 64, width), f32),
        in_specs=[hbm, hbm, smem, vmem],
        out_specs=vmem,
        scratch_shapes=[
            pltpu.VMEM(amplitudes.shape, f32),
            pltpu.VMEM((width, depth), f32),
            pltpu.SemaphoreType.DMA((2,)),
            pltpu.VMEM((BLOCKS, 8, 8, depth), f32),
            pltpu.VMEM((256, 2 * depth), f32),
            pltpu.VMEM((width, 3 * depth), jnp.bfloat16),
            pltpu.VMEM((BLOCKS, 2, tiles, 8, 128), f32),
            sums(BLOCKS), sums(BLOCKS), sums(BLOCKS), sums(BLOCKS), sums(BLOCKS), sums(BLOCKS),
            sums(BLOCKS), sums(5),
            pltpu.VMEM((3, 2, 8, width), f32),
            pltpu.VMEM((3, 2, 8, width), f32),
            pltpu.VMEM((3, 2, 8, width), f32),
            *sems(6), pltpu.SemaphoreType.DMA((3,)),
            *sems(BLOCKS), *sems(BLOCKS), *sems(BLOCKS), *sems(5), *sems(3), *sems(3),
        ],
        compiler_params=pltpu.CompilerParams(
            collective_id=0, has_side_effects=True, vmem_limit_bytes=50 << 20
        ),
    )(amplitudes, integrals.T, occ_irrep, cd_irrep)
    return result.reshape(128, width)


def solution(mesh):
    in_specs = (P("row", None, "col"), P("col", None), P(), P("col"))
    out_specs = P(("row", "col"), None)
    fits = mesh.shape["row"] == 4 and mesh.shape["col"] == 8

    def body(amplitudes, integrals, occ_irrep, cd_irrep):
        paired = fits and amplitudes.shape[:2] == (16, 64) and integrals.shape[1] % 128 == 32
        chosen = paired_body if paired else plain_body
        return chosen(amplitudes, integrals, occ_irrep, cd_irrep)

    return jax.shard_map(body, mesh=mesh, in_specs=in_specs, out_specs=out_specs, check_vma=False)
```
